512 devices in a mesh: slab: 16 (over x_hi, y), sub: 32 (over x_lo, z, core).
Axes of the slice: x: 4 (x_hi: 2, x_lo: 2; x = x_hi * 2 + x_lo), y: 8, z: 8, core: 2. Of those that a mesh axis runs over, the one named last changes fastest.
Arguments:
- offsets: float32 [3, 4, 32, 256, 128], P(None, None, 'slab', 'sub'), may hold values from -0.5 to 0.5
- velocities: float32 [3, 4, 32, 256, 128], P(None, None, 'slab', 'sub'), may hold values from -6 to 6
- chain_label: int32 [4, 32, 256, 128], P(None, 'slab', 'sub'), may hold values from -1 to 31999, as said below
- partners: int32 [2, 4, 32, 256, 128], P(None, None, 'slab', 'sub'), may hold values from 16 to 91, as said below
- anchored: int32 [4, 32, 256, 128], P(None, 'slab', 'sub'), may hold values 0 or 1
Outputs:
- positions: float32 [3, 4, 32, 256, 128], P(None, None, 'slab', 'sub')
- half_velocity: float32 [3, 4, 32, 256, 128], P(None, None, 'slab', 'sub')
- unit_force: float32 [3, 4, 32, 256, 128], P(None, None, 'slab', 'sub')
The draws below stay inside these ranges and needn't reach their ends.
Inputs may be any that keep to these rules, and one draw needn't show every extreme that they name: `chain_label`: beads that carry equal labels within one cell's neighbourhood belong to one loop; -1 marks an empty slot. `partners`: the two codes of a bead name the previous and the next bead of its own loop, in a neighbouring cell, and that bead names it back; every loop is closed. The codes of an empty slot are its own code.
All inputs are finite; a program needn't handle non-finite values. No bound on the sum of `anchored` on one device may be relied on, other than what follows from the above.
Results may differ from the reference program's by a relative error of at most 0.0003.
Values sent between devices are 32-bit elements; how exact they have to be, the bound alone decides.
A program may use at most 64 MiB of HBM per device.

```python
import jax
import jax.numpy as jnp
from jax import lax

SLOTS = 4
DESCENTS = 3
NZ = 128
NX = 32
NY = 256


def draw_offsets(key, part):
    column_x = jnp.arange(NX, dtype=jnp.float32)
    rising = (column_x + 0.5) / NX
    spread = 0.08 + 0.42 * rising
    uniform_base = jnp.clip(0.6 * jax.random.normal(key, (3, SLOTS, NX, NY, NZ), jnp.float32), -1.0, 1.0)
    return uniform_base * spread[None, None, :, None, None]


def loop_layout(key):
    key_first = jax.random.fold_in(key, 11)
    key_gap = jax.random.fold_in(key, 23)
    key_pick = jax.random.fold_in(key, 37)
    first_slot = jax.random.randint(key_first, (NX, NY, NZ), 0, SLOTS, dtype=jnp.int32)
    gap_slot = jax.random.randint(key_gap, (NX, NY, NZ), 1, SLOTS, dtype=jnp.int32)
    second_slot = (first_slot + gap_slot) % SLOTS
    pick = jax.random.randint(key_pick, (NX, NY, NZ), 0, 2, dtype=jnp.int32)
    slot_zero = jnp.where(pick == 0, first_slot, second_slot)
    slot_one = jnp.where(pick == 0, second_slot, first_slot)
    return (slot_zero, slot_one)


def cell_grid():
    grid_x = jnp.broadcast_to(jnp.arange(NX, dtype=jnp.int32)[:, None, None], (NX, NY, NZ))
    grid_y = jnp.broadcast_to(jnp.arange(NY, dtype=jnp.int32)[None, :, None], (NX, NY, NZ))
    grid_z = jnp.broadcast_to(jnp.arange(NZ, dtype=jnp.int32)[None, None, :], (NX, NY, NZ))
    return (grid_x, grid_y, grid_z)


def shifted_grid():
    grid_x, grid_y, grid_z = cell_grid()
    moved_x = (grid_x + (NX - 1)) % NX
    moved_y = (grid_y + (NY - 1)) % NY
    moved_z = (grid_z + (NZ - 1)) % NZ
    return (grid_x, grid_y, grid_z, moved_x, moved_y, moved_z)


def draw_chain_label(key, part):
    slot_zero, slot_one = loop_layout(key)
    grid_x, grid_y, grid_z, moved_x, moved_y, moved_z = shifted_grid()
    block_id = (moved_x // 2 * 7919 + moved_y // 2 * 104729 + moved_z // 4 * 1299) % 16000
    slot_ids = jnp.arange(SLOTS, dtype=jnp.int32)[:, None, None, None]
    label = jnp.where(slot_ids == slot_zero[None], block_id[None] * 2, jnp.where(slot_ids == slot_one[None], block_id[None] * 2 + 1, -1))
    return label.astype(jnp.int32)


def cycle_cell(place):
    quarter = place // 4
    remain = place % 4
    local_z = jnp.where(quarter % 2 == 0, remain, 3 - remain)
    local_x = jnp.where((quarter == 1) | (quarter == 2), 1, 0)
    local_y = jnp.where(quarter >= 2, 1, 0)
    return (local_x, local_y, local_z)


def draw_partners(key, part):
    slot_zero, slot_one = loop_layout(key)
    grid_x, grid_y, grid_z, moved_x, moved_y, moved_z = shifted_grid()
    local_x = moved_x % 2
    local_y = moved_y % 2
    local_z = moved_z % 4
    quarter = jnp.where(local_x == 0, jnp.where(local_y == 0, 0, 3), jnp.where(local_y == 0, 1, 2))
    place = quarter * 4 + jnp.where(quarter % 2 == 0, local_z, 3 - local_z)
    slot_ids = jnp.arange(SLOTS, dtype=jnp.int32)[:, None, None, None]
    codes = []
    for delta in (-1, 1):
        other_x, other_y, other_z = cycle_cell((place + delta) % 16)
        near_x = (grid_x - local_x + other_x + NX) % NX
        near_y = (grid_y - local_y + other_y + NY) % NY
        near_z = (grid_z - local_z + other_z + NZ) % NZ
        cell_code = 9 * (other_x - local_x + 1) + 3 * (other_y - local_y + 1) + (other_z - local_z + 1)
        near_zero = slot_zero[near_x, near_y, near_z]
        near_one = slot_one[near_x, near_y, near_z]
        code = jnp.where(slot_ids == slot_zero[None], cell_code[None] * SLOTS + near_zero[None], jnp.where(slot_ids == slot_one[None], cell_code[None] * SLOTS + near_one[None], 13 * SLOTS + slot_ids))
        codes.append(code)
    return jnp.stack(codes, axis=0).astype(jnp.int32)


def plant(entries, own_key, least, top_value):
    extent = entries.shape
    spot = [jax.random.randint(jax.random.fold_in(own_key, axis), (), 0, extent[axis]) for axis in range(len(extent))]
    entries = entries.at[tuple(spot)].set(least)
    longest = extent.index(max(extent))
    spot[longest] = (spot[longest] + 1) % extent[longest]
    return entries.at[tuple(spot)].set(top_value)


def block_scale(key, dims, cuts, low, largest):
    def one(position, blocks):
        heights = jax.random.uniform(jax.random.fold_in(jax.random.fold_in(key, 6), position), (blocks,), jnp.float32, low / len(cuts), largest / len(cuts))
        return jnp.repeat(jnp.exp(heights), dims[position] // blocks).reshape((-1,) + (1,) * (len(dims) - position - 1))

    loudness = one(*cuts[0])
    for cut in cuts[1:]:
        loudness = loudness * one(*cut)
    return loudness


def centred(stream_key, shape, width, bound, cuts=(), kind=jnp.bfloat16):
    values = jax.random.normal(stream_key, shape, jnp.float32) * width
    if len(cuts) > 0:
        values = block_scale(stream_key, shape, cuts, -0.22, 0.18) * values
    return jnp.clip(values, min=-bound, max=bound).astype(kind)


def setup_inputs(seed: int = 0) -> dict:
    arg_keys = jax.random.split(jax.random.key(seed), 6)
    return {
        "offsets": draw_offsets(jax.random.fold_in(arg_keys[5], 71), 0),
        "velocities": centred(arg_keys[1], (3, SLOTS, NX, NY, NZ), 1.0, 6.0, ((2, 16), (3, 32)), jnp.float32),
        "chain_label": draw_chain_label(jax.random.fold_in(arg_keys[5], 71), 0),
        "partners": draw_partners(jax.random.fold_in(arg_keys[5], 71), 0),
        "anchored": plant((jax.random.randint(arg_keys[4], (SLOTS, NX, NY, NZ), 0, 1000) < 4).astype(jnp.int32), jax.random.fold_in(arg_keys[4], 1), 0, 1),
    }


cell_width = 1.25
cutoff_sq = 2.0 ** (1.0 / 3.0)
soft_floor = 0.64
bond_stiff = 100.0
bond_inv_sq = 1.0 / 9.0
fene_floor = 0.2
time_step = 0.01
half_step = 0.005
half_step_sq = 5e-05
step_length = 0.1
tiny_eps = 1e-06

def pair_force(own_pos, own_label, partner_codes, fetch_pos, fetch_label, keep_chain):
    slot_count = own_pos.shape[1]
    slot_ids = jnp.arange(slot_count, dtype=jnp.int32)
    own_live = own_label >= 0
    summed = jnp.zeros(own_pos.shape, jnp.float32)
    for offset_x in (-1, 0, 1):
        for offset_y in (-1, 0, 1):
            for offset_z in (-1, 0, 1):
                code_base = ((offset_x + 1) * 9 + (offset_y + 1) * 3 + (offset_z + 1)) * slot_count
                other_pos = fetch_pos(offset_x, offset_y, offset_z)
                other_label = fetch_label(offset_x, offset_y, offset_z)
                cell_shift = jnp.array([offset_x, offset_y, offset_z], jnp.float32) * cell_width
                separation = own_pos[:, :, None] - other_pos[:, None] - cell_shift[:, None, None, None, None, None]
                dist_sq = lax.optimization_barrier(jnp.sum(separation * separation, axis=0))
                pair_live = own_live[:, None] & (other_label[None] >= 0)
                if offset_x == 0 and offset_y == 0 and (offset_z == 0):
                    pair_live = pair_live & (slot_ids[:, None, None, None, None] != slot_ids[None, :, None, None, None])
                bond_live = pair_live
                if not keep_chain:
                    pair_live = pair_live & (own_label[:, None] != other_label[None])
                wca_live = pair_live & (dist_sq < cutoff_sq)
                inv_two = 1.0 / jnp.maximum(dist_sq, soft_floor)
                inv_four = inv_two * inv_two
                inv_eight = inv_four * inv_four
                wca_coef = jnp.where(wca_live, 24.0 * (2.0 * inv_eight * inv_four * inv_two - inv_eight), 0.0)
                wanted = (code_base + slot_ids)[None, None, :, None, None, None]
                matches = lax.optimization_barrier(jnp.sum((partner_codes[:, :, None] == wanted).astype(jnp.float32), axis=0))
                fene_coef = -bond_stiff / jnp.maximum(1.0 - dist_sq * bond_inv_sq, fene_floor)
                pair_coef = wca_coef + jnp.where(bond_live, matches, 0.0) * fene_coef
                summed = summed + lax.optimization_barrier(jnp.sum(pair_coef[None] * separation, axis=2))
    return summed

def global_force(positions, labels, partner_codes, keep_chain):
    pos_pad = jnp.concatenate([positions[:, :, -1:], positions, positions[:, :, :1]], axis=2)
    lab_pad = jnp.concatenate([labels[:, -1:], labels, labels[:, :1]], axis=1)

    def plane(plane_index):

        def fetch_pos(offset_x, offset_y, offset_z):
            neighbour = lax.dynamic_slice_in_dim(pos_pad, plane_index + 1 + offset_x, 1, 2)
            return jnp.roll(neighbour, (-offset_y, -offset_z), axis=(3, 4))

        def fetch_label(offset_x, offset_y, offset_z):
            neighbour = lax.dynamic_slice_in_dim(lab_pad, plane_index + 1 + offset_x, 1, 1)
            return jnp.roll(neighbour, (-offset_y, -offset_z), axis=(2, 3))
        own_pos = lax.dynamic_slice_in_dim(positions, plane_index, 1, 2)
        own_label = lax.dynamic_slice_in_dim(labels, plane_index, 1, 1)
        own_codes = lax.dynamic_slice_in_dim(partner_codes, plane_index, 1, 2)
        return pair_force(own_pos, own_label, own_codes, fetch_pos, fetch_label, keep_chain)[:, :, 0]
    planes = lax.map(plane, jnp.arange(NX, dtype=jnp.int32))
    return jnp.moveaxis(planes, 0, 2)

def reference(offsets, velocities, chain_label, partners, anchored):
    free_mask = ((chain_label >= 0) & (anchored == 0)).astype(jnp.float32)
    force_now = global_force(offsets, chain_label, partners, True) * free_mask
    moving = free_mask * velocities
    positions = offsets + (time_step * moving + half_step_sq * force_now)
    half_velocity = moving + half_step * force_now
    inverse = jnp.float32(1.0)
    for descent in range(DESCENTS):
        force_now = global_force(positions, chain_label, partners, False) * free_mask
        peak_force = jnp.sqrt(jnp.max(lax.optimization_barrier(jnp.sum(force_now * force_now, axis=0))))
        inverse = 1.0 / (peak_force + tiny_eps)
        positions = positions + step_length * inverse * force_now
    return (positions, half_velocity, inverse * force_now)
```

```python
import jax
import jax.numpy as jnp
from jax import lax
from jax.experimental import pallas as pl
from jax.experimental.pallas import tpu as pltpu
from jax.sharding import PartitionSpec as P

MESH = pl.DeviceIdType.MESH
SLOTS = 4
PARTS = 12
NSLAB, NSUB = 16, 32
HALF = 16
N1, N2 = 15, 31

cell_width = 1.25
soft_floor = 0.64
bond_stiff = 100.0
time_step = 0.01
half_step = 0.005
half_step_sq = 5e-05
step_length = 0.1
tiny_eps = 1e-06
away = 1.0e4
no_pair = 1.0e3
FORCE_UNIT = 48.0
BOND = -bond_stiff * 9.0 / FORCE_UNIT


def kernel(
    off_in,
    vel_in,
    lab_in,
    par_in,
    anc_in,
    pos_out,
    half_out,
    unit_out,
    off,
    vel,
    lab,
    par,
    anc,
    box,
    labels,
    rows_out,
    rows_in,
    bond,
    floors,
    acc,
    free,
    mine,
    slots,
    load_sem,
    face_send,
    face_recv,
    max_send,
    max_recv,
):
    slab = lax.axis_index("slab")
    sub = lax.axis_index("sub")
    around = (
        (1, 0),
        (-1, 0),
        (0, 1),
        (0, -1),
        (1, 1),
        (1, -1),
        (-1, 1),
        (-1, -1),
    )
    near = [((slab + u + NSLAB) % NSLAB, (sub + v + NSUB) % NSUB) for u, v in around]
    low, part = sub % HALF, sub // HALF
    line = [(slab, part * HALF + (low + d) % HALF) for d in range(1, N1 + 1)]
    place = part * NSLAB + slab
    plane_peers = []
    for d in range(1, N2 + 1):
        there = (place + d) % (NSLAB * 2)
        plane_peers.append((there % NSLAB, (there // NSLAB) * HALF + low))

    barrier = pltpu.get_barrier_semaphore()
    everyone = near + line + plane_peers
    for device in everyone:
        pl.semaphore_signal(barrier, inc=1, device_id=device, device_id_type=MESH)

    loads = [
        pltpu.make_async_copy(source, target, load_sem.at[k])
        for k, (source, target) in enumerate(
            ((off_in, off), (lab_in, lab), (par_in, par), (vel_in, vel), (anc_in, anc))
        )
    ]
    for copy in loads:
        copy.start()

    blank = jnp.zeros((PARTS, 8, 128), jnp.float32)

    def clear(q, carry):
        for e in range(4):
            box[e, q, :, 0:8, :] = blank
            box[e, q, :, 16:24, :] = blank
        labels[q, :, 0:8, :] = blank[:SLOTS]
        labels[q, :, 16:24, :] = blank[:SLOTS]
        return carry

    lax.fori_loop(0, 4, clear, 0)
    rows_out[...] = jnp.zeros(rows_out.shape, jnp.float32)

    loads[0].wait()
    loads[1].wait()
    for p in range(2):
        for j in range(SLOTS):
            label = lab[j, p]
            labels[p + 1, j, 8:16, :] = label.astype(jnp.float32)
            box[0, p + 1, j, 8:16, :] = off[0, j, p] + jnp.where(label < 0, away, 0.0)
            for c in (1, 2):
                box[0, p + 1, c * SLOTS + j, 8:16, :] = off[c, j, p]

    def pack(e):
        for side, row in ((0, 8), (1, 15)):
            for p in range(2):
                for k in range(PARTS):
                    rows_out[e, side, p, k : k + 1, :] = box[e, p + 1, k, row : row + 1, :]

    pack(0)
    for side, row in ((0, 8), (1, 15)):
        for p in range(2):
            for j in range(SLOTS):
                rows_out[0, side, p, PARTS + j : PARTS + j + 1, :] = labels[
                    p + 1, j, row : row + 1, :
                ]

    loads[2].wait()

    def bonds(t, carry):
        p = t // 9
        g = t % 9
        for ez in range(3):
            for j in range(SLOTS):
                wanted = (g * 3 + ez) * SLOTS + j
                for i in range(SLOTS):
                    bond[p, g, ez, j, i] = jnp.where(par[0, i, p] == wanted, BOND, 0.0) + jnp.where(
                        par[1, i, p] == wanted, BOND, 0.0
                    )
        return carry

    lax.fori_loop(0, 18, bonds, 0)
    loads[3].wait()
    loads[4].wait()
    for p in range(2):
        for i in range(SLOTS):
            free[p, i] = jnp.where((lab[i, p] >= 0) & (anc[i, p] == 0), 1.0, 0.0)

    pl.semaphore_wait(barrier, len(everyone))

    def face(e, k, source, target):
        return pltpu.make_async_remote_copy(
            src_ref=source,
            dst_ref=target,
            send_sem=face_send.at[e, k],
            recv_sem=face_recv.at[e, k],
            device_id=near[k % 8],
            device_id_type=MESH,
        )

    def planes(e, p):
        return face(
            e,
            1 - p,
            box.at[e, p + 1, :, 8:16, :],
            box.at[e, 3 - 3 * p, :, 8:16, :],
        )

    def edges(e):
        return [
            face(e, 2, rows_out.at[e, 1], rows_in.at[e, 0, 1:3]),
            face(e, 3, rows_out.at[e, 0], rows_in.at[e, 1, 1:3]),
            face(e, 4, rows_out.at[e, 1, 1], rows_in.at[e, 0, 0]),
            face(e, 5, rows_out.at[e, 0, 1], rows_in.at[e, 1, 0]),
            face(e, 6, rows_out.at[e, 1, 0], rows_in.at[e, 0, 3]),
            face(e, 7, rows_out.at[e, 0, 0], rows_in.at[e, 1, 3]),
        ]

    label_faces = [
        face(0, 9 - p, labels.at[p + 1, :, 8:16, :], labels.at[3 - 3 * p, :, 8:16, :])
        for p in range(2)
    ]
    face_copies = [[planes(e, 0), planes(e, 1)] for e in range(4)]
    edge_copies = [edges(e) for e in range(4)]

    def unpack(e):
        def one(q, carry):
            for side, row in ((0, 7), (1, 16)):
                for k in range(PARTS):
                    box[e, q, k, row : row + 1, :] = rows_in[e, side, q, k : k + 1, :]
            return carry

        lax.fori_loop(0, 4, one, 0)

    def group(e, p, q, ey, fresh):
        ex = (q - p - 1).astype(jnp.float32) * cell_width
        g = 3 * (q - p) + (ey + 1)
        own = [
            [box[e, p + 1, c * SLOTS + i, 8:16, :] for i in range(SLOTS)] for c in range(3)
        ]
        total = [
            [
                jnp.zeros((8, 128), jnp.float32) if fresh else acc[p, c * SLOTS + i]
                for i in range(SLOTS)
            ]
            for c in range(3)
        ]
        own_x = [own[0][i] - ex for i in range(SLOTS)]
        own_y = [own[1][i] - ey * cell_width for i in range(SLOTS)]
        for ez in (-1, 0, 1):
            own_z = [own[2][i] - ez * cell_width for i in range(SLOTS)]
            for j in range(SLOTS):
                other = [box[e, q, c * SLOTS + j, 8 + ey : 16 + ey, :] for c in range(3)]
                if ez != 0:
                    other = [pltpu.roll(o, (-ez) % 128, 1) for o in other]
                for i in range(SLOTS):
                    sx = own_x[i] - other[0]
                    sy = own_y[i] - other[1]
                    sz = own_z[i] - other[2]
                    dist = sx * sx + sy * sy + sz * sz
                    least = soft_floor if e == 0 else floors[p, g, ez + 1, j, i]
                    q1 = pl.reciprocal(jnp.maximum(dist, least), approx=True)
                    q2 = q1 * q1
                    q3 = q2 * q1
                    q4 = q2 * q2
                    push = q4 * jnp.maximum(q3 - 0.5, 0.0)
                    pull = bond[p, g, ez + 1, j, i] * pl.reciprocal(
                        jnp.maximum(9.0 - dist, 1.8), approx=True
                    )
                    coef = push + pull
                    total[0][i] = total[0][i] + coef * sx
                    total[1][i] = total[1][i] + coef * sy
                    total[2][i] = total[2][i] + coef * sz
        for c in range(3):
            for i in range(SLOTS):
                acc[p, c * SLOTS + i] = total[c][i]

    def inner(e):
        def first(p, carry):
            group(e, p, p + 1, 0, True)
            return carry

        def second(p, carry):
            group(e, p, 2 - p, 0, False)
            return carry

        lax.fori_loop(0, 2, first, 0)
        lax.fori_loop(0, 2, second, 0)

    def sides(e):
        def one(t, carry):
            for ey in (-1, 1):
                group(e, t // 2, 1 + t % 2, ey, False)
            return carry

        lax.fori_loop(0, 4, one, 0)

    def outer(e):
        def one(p, carry):
            for ey in (-1, 0, 1):
                group(e, p, 3 * p, ey, False)
            return carry

        lax.fori_loop(0, 2, one, 0)

    def limits():
        def one(t, carry):
            p = t // 3
            for ey in (-1, 0, 1):
                g = 3 * (t % 3) + (ey + 1)
                for ez in (-1, 0, 1):
                    for j in range(SLOTS):
                        other = labels[p + t % 3, j, 8 + ey : 16 + ey, :]
                        if ez != 0:
                            other = pltpu.roll(other, (-ez) % 128, 1)
                        for i in range(SLOTS):
                            floors[p, g, ez + 1, j, i] = jnp.where(
                                labels[p + 1, i, 8:16, :] == other, no_pair, soft_floor
                            )
            return carry

        lax.fori_loop(0, 6, one, 0)

    def global_max(r, value):
        row = jnp.max(value, axis=0, keepdims=True)
        base = 0
        for phase, peers in enumerate((line, plane_peers)):
            mine[r, phase] = row
            copies = [
                pltpu.make_async_remote_copy(
                    src_ref=mine.at[r, phase],
                    dst_ref=slots.at[r, base + k],
                    send_sem=max_send.at[r, base + k],
                    recv_sem=max_recv.at[r, base + k],
                    device_id=device,
                    device_id_type=MESH,
                )
                for k, device in enumerate(peers)
            ]
            for copy in copies:
                copy.start()
            yield copies
            for copy in copies:
                copy.wait_recv()
            row = jnp.maximum(row, jnp.max(slots[r, base : base + len(peers)], axis=0))
            base += len(peers)
        yield jnp.max(row, axis=1, keepdims=True)

    for copy in face_copies[0] + edge_copies[0] + label_faces:
        copy.start()
    inner(0)
    for copy in edge_copies[0]:
        copy.wait_recv()
    unpack(0)
    sides(0)
    for copy in face_copies[0]:
        copy.wait_recv()
    outer(0)
    for p in range(2):
        for c in range(3):
            for i in range(SLOTS):
                k = c * SLOTS + i
                force = acc[p, k] * FORCE_UNIT * free[p, i]
                moving = free[p, i] * vel[c, i, p]
                half_out[c, i, p] = moving + half_step * force
                box[1, p + 1, k, 8:16, :] = box[0, p + 1, k, 8:16, :] + (
                    time_step * moving + half_step_sq * force
                )
        face_copies[1][p].start()
    pack(1)
    for copy in edge_copies[1]:
        copy.start()
    for copy in label_faces:
        copy.wait_recv()

    def label_rows(q, carry):
        for side, row in ((0, 7), (1, 16)):
            for j in range(SLOTS):
                labels[q, j, row : row + 1, :] = rows_in[
                    0, side, q, PARTS + j : PARTS + j + 1, :
                ]
        return carry

    lax.fori_loop(0, 4, label_rows, 0)
    limits()
    inner(1)
    for copy in edge_copies[1]:
        copy.wait_recv()
    unpack(1)
    sides(1)
    for copy in face_copies[1]:
        copy.wait_recv()

    started = face_copies[0] + edge_copies[0] + label_faces + edge_copies[1]
    for r in range(3):
        if r > 0:
            inner(1)
            sides(1)
        outer(1)
        final = r == 2
        peak = jnp.zeros((8, 128), jnp.float32)
        for p in range(2):
            for i in range(SLOTS):
                size = jnp.zeros((8, 128), jnp.float32)
                for c in range(3):
                    k = c * SLOTS + i
                    force = acc[p, k] * FORCE_UNIT * free[p, i]
                    size = size + force * force
                    if final:
                        unit_out[c, i, p] = force
                    else:
                        box[r + 2, p + 1, k, 8:16, :] = force
                peak = jnp.maximum(peak, size)
        steps = global_max(r, peak)
        started += next(steps)
        if not final:
            for copy in face_copies[r + 2]:
                copy.start()
            pack(r + 2)
            for copy in edge_copies[r + 2]:
                copy.start()
            started += face_copies[r + 2] + edge_copies[r + 2]
        started += next(steps)
        if not final:
            for copy in edge_copies[r + 2]:
                copy.wait_recv()
            unpack(r + 2)
            for copy in face_copies[r + 2]:
                copy.wait_recv()
        largest = next(steps)
        inverse = 1.0 / (jnp.sqrt(largest) + tiny_eps)
        scale = step_length * inverse
        if not final:
            if r == 0:
                for copy in face_copies[1]:
                    copy.wait_send()

            def move(q, carry):
                box[1, q] = box[1, q] + scale * box[r + 2, q]
                return carry

            lax.fori_loop(0, 4, move, 0)
        else:
            for p in range(2):
                for c in range(3):
                    for i in range(SLOTS):
                        force = unit_out[c, i, p]
                        place_now = box[1, p + 1, c * SLOTS + i, 8:16, :] + scale * force
                        if c == 0:
                            place_now = jnp.where(lab[i, p] < 0, off[c, i, p], place_now)
                        pos_out[c, i, p] = place_now
                        unit_out[c, i, p] = inverse * force
    for copy in started:
        copy.wait_send()


def shards(offsets, velocities, chain_label, partners, anchored):
    shape = jax.ShapeDtypeStruct(offsets.shape, jnp.float32)
    f32 = jnp.float32
    return tuple(
        pl.pallas_call(
            kernel,
            out_shape=(shape, shape, shape),
            in_specs=[pl.BlockSpec(memory_space=pl.ANY)] * 5,
            out_specs=[pl.BlockSpec(memory_space=pltpu.VMEM)] * 3,
            scratch_shapes=[
                pltpu.VMEM(offsets.shape, f32),
                pltpu.VMEM(velocities.shape, f32),
                pltpu.VMEM(chain_label.shape, jnp.int32),
                pltpu.VMEM(partners.shape, jnp.int32),
                pltpu.VMEM(anchored.shape, jnp.int32),
                pltpu.VMEM((4, 4, PARTS, 24, 128), f32),
                pltpu.VMEM((4, SLOTS, 24, 128), f32),
                pltpu.VMEM((4, 2, 2, 16, 128), f32),
                pltpu.VMEM((4, 2, 4, 16, 128), f32),
                pltpu.VMEM((2, 9, 3, SLOTS, SLOTS, 8, 128), f32),
                pltpu.VMEM((2, 9, 3, SLOTS, SLOTS, 8, 128), f32),
                pltpu.VMEM((2, PARTS, 8, 128), f32),
                pltpu.VMEM((2, SLOTS, 8, 128), f32),
                pltpu.VMEM((3, 2, 1, 128), f32),
                pltpu.VMEM((3, N1 + N2, 1, 128), f32),
                pltpu.SemaphoreType.DMA((5,)),
                pltpu.SemaphoreType.DMA((4, 10)),
                pltpu.SemaphoreType.DMA((4, 10)),
                pltpu.SemaphoreType.DMA((3, N1 + N2)),
                pltpu.SemaphoreType.DMA((3, N1 + N2)),
            ],
            compiler_params=pltpu.CompilerParams(
                collective_id=0, has_side_effects=True, vmem_limit_bytes=24 * 1024 * 1024
            ),
        )(offsets, velocities, chain_label, partners, anchored)
    )


def solution(mesh):
    whole = P(None, None, "slab", "sub", None)
    labels = P(None, "slab", "sub", None)
    return jax.shard_map(
        shards,
        mesh=mesh,
        in_specs=(whole, whole, labels, whole, labels),
        out_specs=(whole, whole, whole),
        check_vma=False,
    )
```

```python
import jax
import jax.numpy as jnp
from jax import lax
from jax.experimental import pallas as pl
from jax.experimental.pallas import tpu as pltpu
from jax.sharding import PartitionSpec as P

MESH = pl.DeviceIdType.MESH
SLOTS = 4
PARTS = 12
NSLAB, NSUB = 16, 32
HALF = 16
N1, N2 = 15, 31

cell_width = 1.25
soft_floor = 0.64
bond_stiff = 100.0
time_step = 0.01
half_step = 0.005
half_step_sq = 5e-05
step_length = 0.1
tiny_eps = 1e-06
away = 1.0e4
no_pair = 1.0e3
FORCE_UNIT = 48.0
BOND = -bond_stiff * 9.0 / FORCE_UNIT


def kernel(
    off_in,
    vel_in,
    lab_in,
    par_in,
    anc_in,
    pos_out,
    half_out,
    unit_out,
    off,
    vel,
    lab,
    par,
    anc,
    box,
    labels,
    rows_out,
    rows_in,
    bond,
    floors,
    acc,
    free,
    mine,
    slots,
    load_sem,
    face_send,
    face_recv,
    max_send,
    max_recv,
):
    slab = lax.axis_index("slab")
    sub = lax.axis_index("sub")
    around = (
        (1, 0),
        (-1, 0),
        (0, 1),
        (0, -1),
        (1, 1),
        (1, -1),
        (-1, 1),
        (-1, -1),
    )
    near = [((slab + u + NSLAB) % NSLAB, (sub + v + NSUB) % NSUB) for u, v in around]
    low, part = sub % HALF, sub // HALF
    line = [(slab, part * HALF + (low + d) % HALF) for d in range(1, N1 + 1)]
    place = part * NSLAB + slab
    plane_peers = []
    for d in range(1, N2 + 1):
        there = (place + d) % (NSLAB * 2)
        plane_peers.append((there % NSLAB, (there // NSLAB) * HALF + low))

    barrier = pltpu.get_barrier_semaphore()
    everyone = plane_peers[::-1] + line + near
    for device in everyone:
        pl.semaphore_signal(barrier, inc=1, device_id=device, device_id_type=MESH)

    loads = [
        pltpu.make_async_copy(source, target, load_sem.at[k])
        for k, (source, target) in enumerate(
            ((off_in, off), (lab_in, lab), (par_in, par), (vel_in, vel), (anc_in, anc))
        )
    ]
    for copy in loads:
        copy.start()

    blank = jnp.zeros((PARTS, 8, 128), jnp.float32)

    def clear(q, carry):
        for e in range(4):
            box[e, q, :, 0:8, :] = blank
            box[e, q, :, 16:24, :] = blank
        labels[q, :, 0:8, :] = blank[:SLOTS]
        labels[q, :, 16:24, :] = blank[:SLOTS]
        return carry

    lax.fori_loop(0, 4, clear, 0)
    rows_out[...] = jnp.zeros(rows_out.shape, jnp.float32)

    loads[0].wait()
    loads[1].wait()
    for p in range(2):
        for j in range(SLOTS):
            label = lab[j, p]
            labels[p + 1, j, 8:16, :] = label.astype(jnp.float32)
            box[0, p + 1, j, 8:16, :] = off[0, j, p] + jnp.where(label < 0, away, 0.0)
            for c in (1, 2):
                box[0, p + 1, c * SLOTS + j, 8:16, :] = off[c, j, p]

    def pack(e, p):
        for side, row in ((0, 8), (1, 15)):
            for k in range(PARTS):
                rows_out[e, side, p, k : k + 1, :] = box[e, p + 1, k, row : row + 1, :]

    pack(0, 0)
    pack(0, 1)
    for side, row in ((0, 8), (1, 15)):
        for p in range(2):
            for j in range(SLOTS):
                rows_out[0, side, p, PARTS + j : PARTS + j + 1, :] = labels[
                    p + 1, j, row : row + 1, :
                ]

    loads[2].wait()

    def bonds(t, carry):
        p = t // 9
        g = t % 9
        for ez in range(3):
            for j in range(SLOTS):
                wanted = (g * 3 + ez) * SLOTS + j
                for i in range(SLOTS):
                    bond[p, g, ez, j, i] = jnp.where(par[0, i, p] == wanted, BOND, 0.0) + jnp.where(
                        par[1, i, p] == wanted, BOND, 0.0
                    )
        return carry

    lax.fori_loop(0, 18, bonds, 0)
    loads[3].wait()
    loads[4].wait()
    for p in range(2):
        for i in range(SLOTS):
            free[p, i] = jnp.where((lab[i, p] >= 0) & (anc[i, p] == 0), 1.0, 0.0)

    pl.semaphore_wait(barrier, len(everyone))

    def send(e, k, to, source, target):
        return pltpu.make_async_remote_copy(
            src_ref=source,
            dst_ref=target,
            send_sem=face_send.at[e, k],
            recv_sem=face_recv.at[e, k],
            device_id=near[around.index(to)],
            device_id_type=MESH,
        )

    def face(e, p):
        x = 2 * p - 1
        own, far = box.at[e, p + 1, :, 8:16, :], box.at[e, 3 - 3 * p, :, 8:16, :]
        return send(e, 5 * p, (x, 0), own, far)

    def edges(e, p):
        x, q = 2 * p - 1, 3 - 3 * p
        out = []
        for side, y in ((0, -1), (1, 1)):
            rows, here = rows_out.at[e, side, p], rows_in.at[e, 1 - side]
            out.append(send(e, 5 * p + 1 + side, (0, y), rows, here.at[p + 1]))
            out.append(send(e, 5 * p + 3 + side, (x, y), rows, here.at[q]))
        return out

    label_faces = [
        send(
            0,
            10 + p,
            (2 * p - 1, 0),
            labels.at[p + 1, :, 8:16, :],
            labels.at[3 - 3 * p, :, 8:16, :],
        )
        for p in range(2)
    ]
    face_copies = [[face(e, p) for p in range(2)] for e in range(4)]
    edge_copies = [[edges(e, p) for p in range(2)] for e in range(4)]

    def unpack(e, p):
        def one(t, carry):
            q = (1 + 2 * t) if p == 0 else (2 - 2 * t)
            for side, row in ((0, 7), (1, 16)):
                for k in range(PARTS):
                    box[e, q, k, row : row + 1, :] = rows_in[e, side, q, k : k + 1, :]
            return carry

        lax.fori_loop(0, 2, one, 0)

    def group(e, p, q, ey, fresh):
        ex = (q - p - 1).astype(jnp.float32) * cell_width
        g = 3 * (q - p) + (ey + 1)
        own = [
            [box[e, p + 1, c * SLOTS + i, 8:16, :] for i in range(SLOTS)] for c in range(3)
        ]
        total = [
            [
                jnp.zeros((8, 128), jnp.float32) if fresh else acc[p, c * SLOTS + i]
                for i in range(SLOTS)
            ]
            for c in range(3)
        ]
        own_x = [own[0][i] - ex for i in range(SLOTS)]
        own_y = [own[1][i] - ey * cell_width for i in range(SLOTS)]
        for ez in (-1, 0, 1):
            own_z = [own[2][i] - ez * cell_width for i in range(SLOTS)]
            for j in range(SLOTS):
                other = [box[e, q, c * SLOTS + j, 8 + ey : 16 + ey, :] for c in range(3)]
                if ez != 0:
                    other = [pltpu.roll(o, (-ez) % 128, 1) for o in other]
                for i in range(SLOTS):
                    sx = own_x[i] - other[0]
                    sy = own_y[i] - other[1]
                    sz = own_z[i] - other[2]
                    dist = sx * sx + sy * sy + sz * sz
                    least = soft_floor if e == 0 else floors[p, g, ez + 1, j, i]
                    q1 = pl.reciprocal(jnp.maximum(dist, least), approx=True)
                    q2 = q1 * q1
                    q3 = q2 * q1
                    q4 = q2 * q2
                    push = q4 * jnp.maximum(q3 - 0.5, 0.0)
                    pull = bond[p, g, ez + 1, j, i] * pl.reciprocal(
                        jnp.maximum(9.0 - dist, 1.8), approx=True
                    )
                    coef = push + pull
                    total[0][i] = total[0][i] + coef * sx
                    total[1][i] = total[1][i] + coef * sy
                    total[2][i] = total[2][i] + coef * sz
        for c in range(3):
            for i in range(SLOTS):
                acc[p, c * SLOTS + i] = total[c][i]

    def inner(e):
        def first(p, carry):
            group(e, p, p + 1, 0, True)
            return carry

        def second(p, carry):
            group(e, p, 2 - p, 0, False)
            return carry

        lax.fori_loop(0, 2, first, 0)
        lax.fori_loop(0, 2, second, 0)

    def sides(e, pairs):
        def one(t, carry):
            p, q = pairs(t)
            for ey in (-1, 1):
                group(e, p, q, ey, False)
            return carry

        return one

    def outer(e, p):
        for ey in (-1, 0, 1):
            group(e, p, 3 * p, ey, False)

    def limits():
        def one(t, carry):
            p = t // 3
            for ey in (-1, 0, 1):
                g = 3 * (t % 3) + (ey + 1)
                for ez in (-1, 0, 1):
                    for j in range(SLOTS):
                        other = labels[p + t % 3, j, 8 + ey : 16 + ey, :]
                        if ez != 0:
                            other = pltpu.roll(other, (-ez) % 128, 1)
                        for i in range(SLOTS):
                            floors[p, g, ez + 1, j, i] = jnp.where(
                                labels[p + 1, i, 8:16, :] == other, no_pair, soft_floor
                            )
            return carry

        lax.fori_loop(0, 6, one, 0)

    def global_max(r, value):
        row = jnp.max(value, axis=0, keepdims=True)
        base = 0
        for phase, peers in enumerate((line, plane_peers)):
            mine[r, phase] = row
            copies = [
                pltpu.make_async_remote_copy(
                    src_ref=mine.at[r, phase],
                    dst_ref=slots.at[r, base + k],
                    send_sem=max_send.at[r, base + k],
                    recv_sem=max_recv.at[r, base + k],
                    device_id=device,
                    device_id_type=MESH,
                )
                for k, device in enumerate(peers)
            ]
            for copy in copies:
                copy.start()
            yield copies
            for copy in copies:
                copy.wait_recv()
            row = jnp.maximum(row, jnp.max(slots[r, base : base + len(peers)], axis=0))
            base += len(peers)
        yield jnp.max(row, axis=1, keepdims=True)

    for copy in face_copies[0] + edge_copies[0][0] + edge_copies[0][1] + label_faces:
        copy.start()
    inner(0)
    for p in range(2):
        for copy in edge_copies[0][p]:
            copy.wait_recv()
        unpack(0, p)
    for p in range(2):
        lax.fori_loop(0, 2, sides(0, lambda t: (jnp.int32(p), 1 + t)), 0)
        face_copies[0][1 - p].wait_recv()
        outer(0, jnp.int32(p))
        for c in range(3):
            for i in range(SLOTS):
                k = c * SLOTS + i
                force = acc[p, k] * FORCE_UNIT * free[p, i]
                moving = free[p, i] * vel[c, i, p]
                half_out[c, i, p] = moving + half_step * force
                box[1, p + 1, k, 8:16, :] = box[0, p + 1, k, 8:16, :] + (
                    time_step * moving + half_step_sq * force
                )
        face_copies[1][p].start()
        pack(1, p)
        for copy in edge_copies[1][p]:
            copy.start()
    for copy in label_faces:
        copy.wait_recv()

    def label_rows(q, carry):
        for side, row in ((0, 7), (1, 16)):
            for j in range(SLOTS):
                labels[q, j, row : row + 1, :] = rows_in[
                    0, side, q, PARTS + j : PARTS + j + 1, :
                ]
        return carry

    lax.fori_loop(0, 4, label_rows, 0)
    limits()
    inner(1)
    for p in range(2):
        for copy in edge_copies[1][p]:
            copy.wait_recv()
        unpack(1, p)
        lax.fori_loop(0, 2, sides(1, lambda t: (t, jnp.int32(p + 1))), 0)
        face_copies[1][p].wait_recv()
        outer(1, jnp.int32(1 - p))

    started = face_copies[0] + label_faces
    for e in range(2):
        started += edge_copies[e][0] + edge_copies[e][1]
    for r in range(3):
        if r > 0:
            inner(1)
            lax.fori_loop(0, 4, sides(1, lambda t: (t // 2, 1 + t % 2)), 0)

            def far(p, carry):
                outer(1, p)
                return carry

            lax.fori_loop(0, 2, far, 0)
        final = r == 2
        peak = jnp.zeros((8, 128), jnp.float32)
        for p in range(2):
            for i in range(SLOTS):
                size = jnp.zeros((8, 128), jnp.float32)
                for c in range(3):
                    k = c * SLOTS + i
                    force = acc[p, k] * FORCE_UNIT * free[p, i]
                    size = size + force * force
                    if final:
                        unit_out[c, i, p] = force
                    else:
                        box[r + 2, p + 1, k, 8:16, :] = force
                peak = jnp.maximum(peak, size)
        steps = global_max(r, peak)
        started += next(steps)
        if not final:
            for p in range(2):
                face_copies[r + 2][p].start()
                pack(r + 2, p)
                for copy in edge_copies[r + 2][p]:
                    copy.start()
                started += [face_copies[r + 2][p]] + edge_copies[r + 2][p]
        started += next(steps)
        if not final:
            for p in range(2):
                for copy in edge_copies[r + 2][p]:
                    copy.wait_recv()
                unpack(r + 2, p)
                face_copies[r + 2][p].wait_recv()
        largest = next(steps)
        inverse = 1.0 / (jnp.sqrt(largest) + tiny_eps)
        scale = step_length * inverse
        if not final:
            if r == 0:
                for copy in face_copies[1]:
                    copy.wait_send()

            def move(q, carry):
                box[1, q] = box[1, q] + scale * box[r + 2, q]
                return carry

            lax.fori_loop(0, 4, move, 0)
        else:
            for p in range(2):
                for c in range(3):
                    for i in range(SLOTS):
                        force = unit_out[c, i, p]
                        place_now = box[1, p + 1, c * SLOTS + i, 8:16, :] + scale * force
                        if c == 0:
                            place_now = jnp.where(lab[i, p] < 0, off[c, i, p], place_now)
                        pos_out[c, i, p] = place_now
                        unit_out[c, i, p] = inverse * force
    for copy in started:
        copy.wait_send()


def store(pos, half, unit, pos_out, half_out, unit_out, sem):
    copies = [
        pltpu.make_async_copy(source, target, sem.at[k])
        for k, (source, target) in enumerate(
            ((pos, pos_out), (half, half_out), (unit, unit_out))
        )
    ]
    for copy in copies:
        copy.start()
    for copy in copies:
        copy.wait()


def shards(offsets, velocities, chain_label, partners, anchored):
    f32 = jnp.float32
    shape = offsets.shape
    parts = pl.pallas_call(
        kernel,
        out_shape=(pltpu.VMEM(shape, f32),) * 3,
        in_specs=[pl.BlockSpec(memory_space=pl.ANY)] * 5,
        out_specs=[pl.BlockSpec(memory_space=pltpu.VMEM)] * 3,
        scratch_shapes=[
            pltpu.VMEM(shape, f32),
            pltpu.VMEM(shape, f32),
            pltpu.VMEM(chain_label.shape, jnp.int32),
            pltpu.VMEM(partners.shape, jnp.int32),
            pltpu.VMEM(anchored.shape, jnp.int32),
            pltpu.VMEM((4, 4, PARTS, 24, 128), f32),
            pltpu.VMEM((4, SLOTS, 24, 128), f32),
            pltpu.VMEM((4, 2, 2, 16, 128), f32),
            pltpu.VMEM((4, 2, 4, 16, 128), f32),
            pltpu.VMEM((2, 9, 3, SLOTS, SLOTS, 8, 128), f32),
            pltpu.VMEM((2, 9, 3, SLOTS, SLOTS, 8, 128), f32),
            pltpu.VMEM((2, PARTS, 8, 128), f32),
            pltpu.VMEM((2, SLOTS, 8, 128), f32),
            pltpu.VMEM((3, 2, 1, 128), f32),
            pltpu.VMEM((3, N1 + N2, 1, 128), f32),
            pltpu.SemaphoreType.DMA((5,)),
            pltpu.SemaphoreType.DMA((4, 12)),
            pltpu.SemaphoreType.DMA((4, 12)),
            pltpu.SemaphoreType.DMA((3, N1 + N2)),
            pltpu.SemaphoreType.DMA((3, N1 + N2)),
        ],
        compiler_params=pltpu.CompilerParams(
            collective_id=0, has_side_effects=True, vmem_limit_bytes=60 * 1024 * 1024
        ),
    )(offsets, velocities, chain_label, partners, anchored)
    return tuple(
        pl.pallas_call(
            store,
            out_shape=(jax.ShapeDtypeStruct(shape, f32),) * 3,
            in_specs=[pl.BlockSpec(memory_space=pl.ANY)] * 3,
            out_specs=[pl.BlockSpec(memory_space=pl.ANY)] * 3,
            scratch_shapes=[pltpu.SemaphoreType.DMA((3,))],
            compiler_params=pltpu.CompilerParams(vmem_limit_bytes=1024 * 1024),
        )(*parts)
    )


def solution(mesh):
    whole = P(None, None, "slab", "sub", None)
    labels = P(None, "slab", "sub", None)
    return jax.shard_map(
        shards,
        mesh=mesh,
        in_specs=(whole, whole, labels, whole, labels),
        out_specs=(whole, whole, whole),
        check_vma=False,
    )
```

```python
import jax
import jax.numpy as jnp
from jax import lax
from jax.experimental import pallas as pl
from jax.experimental.pallas import tpu as pltpu
from jax.sharding import PartitionSpec as P

MESH = pl.DeviceIdType.MESH
SLOTS = 4
PARTS = 12
NSLAB, NSUB = 16, 32


def hops(offset):
    dx, dy, dz, _ = offset
    return min(dx, 4 - dx) + min(dy, 8 - dy) + min(dz, 8 - dz)


LINE = [(0, 0, dz, dc) for dz in range(8) for dc in range(2) if dz + dc > 0]
PLANE = [(dx, dy, 0, 0) for dx in range(4) for dy in range(8) if dx + dy > 0]
FAR = [
    (dx, dy, dz, dc)
    for dx, dy, _, _ in PLANE
    for dz in (3, 4, 5)
    for dc in range(2)
    if hops((dx, dy, dz, dc)) >= 9
]
PEERS = LINE + PLANE + FAR
ROUTE = sorted(range(len(PEERS)), key=lambda k: -hops(PEERS[k]))
LINE_KEYS = [k for k in ROUTE if k < len(LINE)]
PLANE_KEYS = [k for k in ROUTE if len(LINE) <= k < len(LINE) + len(PLANE)]
FAR_KEYS = [k for k in ROUTE if k >= len(LINE) + len(PLANE)]

cell_width = 1.25
soft_floor = 0.64
bond_stiff = 100.0
time_step = 0.01
half_step = 0.005
half_step_sq = 5e-05
step_length = 0.1
tiny_eps = 1e-06
away = 1.0e4
no_pair = 1.0e3
FORCE_UNIT = 48.0
BOND = -bond_stiff * 9.0 / FORCE_UNIT


def kernel(
    off_in,
    vel_in,
    lab_in,
    par_in,
    anc_in,
    pos_out,
    half_out,
    unit_out,
    off,
    vel,
    lab,
    par,
    anc,
    box,
    labels,
    rows_out,
    rows_in,
    bond,
    floors,
    acc,
    free,
    mine,
    slots,
    load_sem,
    face_send,
    face_recv,
    max_send,
    max_recv,
):
    slab = lax.axis_index("slab")
    sub = lax.axis_index("sub")
    around = (
        (1, 0),
        (-1, 0),
        (0, 1),
        (0, -1),
        (1, 1),
        (1, -1),
        (-1, 1),
        (-1, -1),
    )
    near = [((slab + u + NSLAB) % NSLAB, (sub + v + NSUB) % NSUB) for u, v in around]
    x, y = (slab // 8) * 2 + sub // 16, slab % 8
    z, core = (sub // 2) % 8, sub % 2
    peers = []
    for dx, dy, dz, dc in PEERS:
        there = (x + dx) % 4
        z_core = ((z + dz) % 8) * 2 + (core + dc) % 2
        peers.append(((there // 2) * 8 + (y + dy) % 8, (there % 2) * 16 + z_core))

    barrier = pltpu.get_barrier_semaphore()
    everyone = [peers[k] for k in ROUTE] + near
    for device in everyone:
        pl.semaphore_signal(barrier, inc=1, device_id=device, device_id_type=MESH)

    loads = [
        pltpu.make_async_copy(source, target, load_sem.at[k])
        for k, (source, target) in enumerate(
            ((off_in, off), (lab_in, lab), (par_in, par), (vel_in, vel), (anc_in, anc))
        )
    ]
    for copy in loads:
        copy.start()

    blank = jnp.zeros((PARTS, 8, 128), jnp.float32)

    def clear(q, carry):
        for e in range(4):
            box[e, q, :, 0:8, :] = blank
            box[e, q, :, 16:24, :] = blank
        labels[q, :, 0:8, :] = blank[:SLOTS]
        labels[q, :, 16:24, :] = blank[:SLOTS]
        return carry

    lax.fori_loop(0, 4, clear, 0)
    rows_out[...] = jnp.zeros(rows_out.shape, jnp.float32)

    loads[0].wait()
    loads[1].wait()
    for p in range(2):
        for j in range(SLOTS):
            label = lab[j, p]
            labels[p + 1, j, 8:16, :] = label.astype(jnp.float32)
            box[0, p + 1, j, 8:16, :] = off[0, j, p] + jnp.where(label < 0, away, 0.0)
            for c in (1, 2):
                box[0, p + 1, c * SLOTS + j, 8:16, :] = off[c, j, p]

    def pack(e, p):
        for side, row in ((0, 8), (1, 15)):
            for k in range(PARTS):
                rows_out[e, side, p, k : k + 1, :] = box[e, p + 1, k, row : row + 1, :]

    pack(0, 0)
    pack(0, 1)
    for side, row in ((0, 8), (1, 15)):
        for p in range(2):
            for j in range(SLOTS):
                rows_out[0, side, p, PARTS + j : PARTS + j + 1, :] = labels[
                    p + 1, j, row : row + 1, :
                ]

    loads[2].wait()

    def bonds(t, carry):
        p = t // 9
        g = t % 9
        for ez in range(3):
            for j in range(SLOTS):
                wanted = (g * 3 + ez) * SLOTS + j
                for i in range(SLOTS):
                    bond[p, g, ez, j, i] = jnp.where(par[0, i, p] == wanted, BOND, 0.0) + jnp.where(
                        par[1, i, p] == wanted, BOND, 0.0
                    )
        return carry

    lax.fori_loop(0, 18, bonds, 0)
    loads[3].wait()
    loads[4].wait()
    for p in range(2):
        for i in range(SLOTS):
            free[p, i] = jnp.where((lab[i, p] >= 0) & (anc[i, p] == 0), 1.0, 0.0)

    pl.semaphore_wait(barrier, len(everyone))

    def send(e, k, to, source, target):
        return pltpu.make_async_remote_copy(
            src_ref=source,
            dst_ref=target,
            send_sem=face_send.at[e, k],
            recv_sem=face_recv.at[e, k],
            device_id=near[around.index(to)],
            device_id_type=MESH,
        )

    def face(e, p):
        x = 2 * p - 1
        own, far = box.at[e, p + 1, :, 8:16, :], box.at[e, 3 - 3 * p, :, 8:16, :]
        return send(e, 5 * p, (x, 0), own, far)

    def edges(e, p):
        x, q = 2 * p - 1, 3 - 3 * p
        out = []
        for side, y in ((0, -1), (1, 1)):
            rows, here = rows_out.at[e, side, p], rows_in.at[e, 1 - side]
            out.append(send(e, 5 * p + 1 + side, (0, y), rows, here.at[p + 1]))
            out.append(send(e, 5 * p + 3 + side, (x, y), rows, here.at[q]))
        return out

    label_faces = [
        send(
            0,
            10 + p,
            (2 * p - 1, 0),
            labels.at[p + 1, :, 8:16, :],
            labels.at[3 - 3 * p, :, 8:16, :],
        )
        for p in range(2)
    ]
    face_copies = [[face(e, p) for p in range(2)] for e in range(4)]
    edge_copies = [[edges(e, p) for p in range(2)] for e in range(4)]

    def unpack(e, p):
        def one(t, carry):
            q = (1 + 2 * t) if p == 0 else (2 - 2 * t)
            for side, row in ((0, 7), (1, 16)):
                for k in range(PARTS):
                    box[e, q, k, row : row + 1, :] = rows_in[e, side, q, k : k + 1, :]
            return carry

        lax.fori_loop(0, 2, one, 0)

    def group(e, p, q, ey, fresh):
        ex = (q - p - 1).astype(jnp.float32) * cell_width
        g = 3 * (q - p) + (ey + 1)
        own = [
            [box[e, p + 1, c * SLOTS + i, 8:16, :] for i in range(SLOTS)] for c in range(3)
        ]
        total = [
            [
                jnp.zeros((8, 128), jnp.float32) if fresh else acc[p, c * SLOTS + i]
                for i in range(SLOTS)
            ]
            for c in range(3)
        ]
        own_x = [own[0][i] - ex for i in range(SLOTS)]
        own_y = [own[1][i] - ey * cell_width for i in range(SLOTS)]
        for ez in (-1, 0, 1):
            own_z = [own[2][i] - ez * cell_width for i in range(SLOTS)]
            for j in range(SLOTS):
                other = [box[e, q, c * SLOTS + j, 8 + ey : 16 + ey, :] for c in range(3)]
                if ez != 0:
                    other = [pltpu.roll(o, (-ez) % 128, 1) for o in other]
                for i in range(SLOTS):
                    sx = own_x[i] - other[0]
                    sy = own_y[i] - other[1]
                    sz = own_z[i] - other[2]
                    dist = sx * sx + sy * sy + sz * sz
                    least = soft_floor if e == 0 else floors[p, g, ez + 1, j, i]
                    q1 = pl.reciprocal(jnp.maximum(dist, least), approx=True)
                    q2 = q1 * q1
                    q3 = q2 * q1
                    q4 = q2 * q2
                    push = q4 * jnp.maximum(q3 - 0.5, 0.0)
                    pull = bond[p, g, ez + 1, j, i] * pl.reciprocal(
                        jnp.maximum(9.0 - dist, 1.8), approx=True
                    )
                    coef = push + pull
                    total[0][i] = total[0][i] + coef * sx
                    total[1][i] = total[1][i] + coef * sy
                    total[2][i] = total[2][i] + coef * sz
        for c in range(3):
            for i in range(SLOTS):
                acc[p, c * SLOTS + i] = total[c][i]

    def inner(e):
        def first(p, carry):
            group(e, p, p + 1, 0, True)
            return carry

        def second(p, carry):
            group(e, p, 2 - p, 0, False)
            return carry

        lax.fori_loop(0, 2, first, 0)
        lax.fori_loop(0, 2, second, 0)

    def sides(e, pairs):
        def one(t, carry):
            p, q = pairs(t)
            for ey in (-1, 1):
                group(e, p, q, ey, False)
            return carry

        return one

    def outer(e, p):
        for ey in (-1, 0, 1):
            group(e, p, 3 * p, ey, False)

    def limits():
        def one(t, carry):
            p = t // 3
            for ey in (-1, 0, 1):
                g = 3 * (t % 3) + (ey + 1)
                for ez in (-1, 0, 1):
                    for j in range(SLOTS):
                        other = labels[p + t % 3, j, 8 + ey : 16 + ey, :]
                        if ez != 0:
                            other = pltpu.roll(other, (-ez) % 128, 1)
                        for i in range(SLOTS):
                            floors[p, g, ez + 1, j, i] = jnp.where(
                                labels[p + 1, i, 8:16, :] == other, no_pair, soft_floor
                            )
            return carry

        lax.fori_loop(0, 6, one, 0)

    def global_max(r, value):
        row = jnp.max(value, axis=0, keepdims=True)
        waiting = {}

        def tell(stage, keys):
            mine[r, stage] = row
            for k in keys:
                waiting[k] = pltpu.make_async_remote_copy(
                    src_ref=mine.at[r, stage],
                    dst_ref=slots.at[r, k],
                    send_sem=max_send.at[r, k],
                    recv_sem=max_recv.at[r, k],
                    device_id=peers[k],
                    device_id_type=MESH,
                )
                waiting[k].start()

        tell(0, LINE_KEYS + FAR_KEYS)
        yield []
        for stage, (nearest, farthest) in enumerate(((0, 2), (3, 3), (4, 4))):
            heard = [k for k in LINE_KEYS if nearest <= hops(PEERS[k]) <= farthest]
            for k in heard:
                waiting[k].wait_recv()
            for k in heard:
                row = jnp.maximum(row, slots[r, k])
            tell(
                stage + 1,
                [
                    k
                    for k in PLANE_KEYS
                    if hops(PEERS[k]) == 6 - stage or (stage == 2 and hops(PEERS[k]) < 4)
                ],
            )
        yield list(waiting.values())
        for k in PLANE_KEYS[::-1] + FAR_KEYS:
            waiting[k].wait_recv()
        row = jnp.maximum(row, jnp.max(slots[r, len(LINE) :], axis=0))
        yield jnp.max(row, axis=1, keepdims=True)

    for copy in face_copies[0] + edge_copies[0][0] + edge_copies[0][1] + label_faces:
        copy.start()
    inner(0)
    for p in range(2):
        for copy in edge_copies[0][p]:
            copy.wait_recv()
        unpack(0, p)
    for p in range(2):
        lax.fori_loop(0, 2, sides(0, lambda t: (jnp.int32(p), 1 + t)), 0)
        face_copies[0][1 - p].wait_recv()
        outer(0, jnp.int32(p))
        for c in range(3):
            for i in range(SLOTS):
                k = c * SLOTS + i
                force = acc[p, k] * FORCE_UNIT * free[p, i]
                moving = free[p, i] * vel[c, i, p]
                half_out[c, i, p] = moving + half_step * force
                box[1, p + 1, k, 8:16, :] = box[0, p + 1, k, 8:16, :] + (
                    time_step * moving + half_step_sq * force
                )
        face_copies[1][p].start()
        pack(1, p)
        for copy in edge_copies[1][p]:
            copy.start()
    for copy in label_faces:
        copy.wait_recv()

    def label_rows(q, carry):
        for side, row in ((0, 7), (1, 16)):
            for j in range(SLOTS):
                labels[q, j, row : row + 1, :] = rows_in[
                    0, side, q, PARTS + j : PARTS + j + 1, :
                ]
        return carry

    lax.fori_loop(0, 4, label_rows, 0)
    limits()
    inner(1)
    for p in range(2):
        for copy in edge_copies[1][p]:
            copy.wait_recv()
        unpack(1, p)
        lax.fori_loop(0, 2, sides(1, lambda t: (t, jnp.int32(p + 1))), 0)
        face_copies[1][p].wait_recv()
        outer(1, jnp.int32(1 - p))

    started = face_copies[0] + label_faces
    for e in range(2):
        started += edge_copies[e][0] + edge_copies[e][1]
    for r in range(3):
        if r > 0:
            inner(1)
            lax.fori_loop(0, 4, sides(1, lambda t: (t // 2, 1 + t % 2)), 0)

            def far(p, carry):
                outer(1, p)
                return carry

            lax.fori_loop(0, 2, far, 0)
        final = r == 2
        peak = jnp.zeros((8, 128), jnp.float32)
        for p in range(2):
            for i in range(SLOTS):
                size = jnp.zeros((8, 128), jnp.float32)
                for c in range(3):
                    k = c * SLOTS + i
                    force = acc[p, k] * FORCE_UNIT * free[p, i]
                    size = size + force * force
                    if final:
                        unit_out[c, i, p] = force
                    else:
                        box[r + 2, p + 1, k, 8:16, :] = force
                peak = jnp.maximum(peak, size)
        steps = global_max(r, peak)
        started += next(steps)
        if not final:
            for p in range(2):
                face_copies[r + 2][p].start()
                pack(r + 2, p)
                for copy in edge_copies[r + 2][p]:
                    copy.start()
                started += [face_copies[r + 2][p]] + edge_copies[r + 2][p]
        started += next(steps)
        if not final:
            for p in range(2):
                for copy in edge_copies[r + 2][p]:
                    copy.wait_recv()
                unpack(r + 2, p)
                face_copies[r + 2][p].wait_recv()
        largest = next(steps)
        inverse = 1.0 / (jnp.sqrt(largest) + tiny_eps)
        scale = step_length * inverse
        if not final:
            if r == 0:
                for copy in face_copies[1]:
                    copy.wait_send()

            def move(q, carry):
                box[1, q] = box[1, q] + scale * box[r + 2, q]
                return carry

            lax.fori_loop(0, 4, move, 0)
        else:
            for p in range(2):
                for c in range(3):
                    for i in range(SLOTS):
                        force = unit_out[c, i, p]
                        place_now = box[1, p + 1, c * SLOTS + i, 8:16, :] + scale * force
                        if c == 0:
                            place_now = jnp.where(lab[i, p] < 0, off[c, i, p], place_now)
                        pos_out[c, i, p] = place_now
                        unit_out[c, i, p] = inverse * force
    for copy in started:
        copy.wait_send()


def store(pos, half, unit, pos_out, half_out, unit_out, sem):
    copies = [
        pltpu.make_async_copy(source, target, sem.at[k])
        for k, (source, target) in enumerate(
            ((pos, pos_out), (half, half_out), (unit, unit_out))
        )
    ]
    for copy in copies:
        copy.start()
    for copy in copies:
        copy.wait()


def shards(offsets, velocities, chain_label, partners, anchored):
    f32 = jnp.float32
    shape = offsets.shape
    parts = pl.pallas_call(
        kernel,
        out_shape=(pltpu.VMEM(shape, f32),) * 3,
        in_specs=[pl.BlockSpec(memory_space=pl.ANY)] * 5,
        out_specs=[pl.BlockSpec(memory_space=pltpu.VMEM)] * 3,
        scratch_shapes=[
            pltpu.VMEM(shape, f32),
            pltpu.VMEM(shape, f32),
            pltpu.VMEM(chain_label.shape, jnp.int32),
            pltpu.VMEM(partners.shape, jnp.int32),
            pltpu.VMEM(anchored.shape, jnp.int32),
            pltpu.VMEM((4, 4, PARTS, 24, 128), f32),
            pltpu.VMEM((4, SLOTS, 24, 128), f32),
            pltpu.VMEM((4, 2, 2, 16, 128), f32),
            pltpu.VMEM((4, 2, 4, 16, 128), f32),
            pltpu.VMEM((2, 9, 3, SLOTS, SLOTS, 8, 128), f32),
            pltpu.VMEM((2, 9, 3, SLOTS, SLOTS, 8, 128), f32),
            pltpu.VMEM((2, PARTS, 8, 128), f32),
            pltpu.VMEM((2, SLOTS, 8, 128), f32),
            pltpu.VMEM((3, 4, 1, 128), f32),
            pltpu.VMEM((3, len(PEERS), 1, 128), f32),
            pltpu.SemaphoreType.DMA((5,)),
            pltpu.SemaphoreType.DMA((4, 12)),
            pltpu.SemaphoreType.DMA((4, 12)),
            pltpu.SemaphoreType.DMA((3, len(PEERS))),
            pltpu.SemaphoreType.DMA((3, len(PEERS))),
        ],
        compiler_params=pltpu.CompilerParams(
            collective_id=0, has_side_effects=True, vmem_limit_bytes=60 * 1024 * 1024
        ),
    )(offsets, velocities, chain_label, partners, anchored)
    return tuple(
        pl.pallas_call(
            store,
            out_shape=(jax.ShapeDtypeStruct(shape, f32),) * 3,
            in_specs=[pl.BlockSpec(memory_space=pl.ANY)] * 3,
            out_specs=[pl.BlockSpec(memory_space=pl.ANY)] * 3,
            scratch_shapes=[pltpu.SemaphoreType.DMA((3,))],
            compiler_params=pltpu.CompilerParams(vmem_limit_bytes=1024 * 1024),
        )(*parts)
    )


def solution(mesh):
    whole = P(None, None, "slab", "sub", None)
    labels = P(None, "slab", "sub", None)
    return jax.shard_map(
        shards,
        mesh=mesh,
        in_specs=(whole, whole, labels, whole, labels),
        out_specs=(whole, whole, whole),
        check_vma=False,
    )
```

```python
import jax
import jax.numpy as jnp
from jax import lax
from jax.experimental import pallas as pl
from jax.experimental.pallas import tpu as pltpu
from jax.sharding import PartitionSpec as P

MESH = pl.DeviceIdType.MESH
SLOTS = 4
PARTS = 12
NSLAB, NSUB = 16, 32
HALF = 16
N1, N2 = 15, 31

LINE_STEPS = sorted(range(1, N1 + 1), key=lambda d: -min(d, HALF - d))
PLANE_STEPS = sorted(range(1, N2 + 1), key=lambda d: -min(d % 8, 8 - d % 8))

cell_width = 1.25
soft_floor = 0.64
bond_stiff = 100.0
time_step = 0.01
half_step = 0.005
half_step_sq = 5e-05
step_length = 0.1
tiny_eps = 1e-06
away = 1.0e4
no_pair = 1.0e3
FORCE_UNIT = 48.0
BOND = -bond_stiff * 9.0 / FORCE_UNIT


def kernel(
    off_in,
    vel_in,
    lab_in,
    par_in,
    anc_in,
    pos_out,
    half_out,
    unit_out,
    off,
    vel,
    lab,
    par,
    anc,
    box,
    labels,
    rows_out,
    rows_in,
    bond,
    floors,
    acc,
    free,
    mine,
    slots,
    load_sem,
    face_send,
    face_recv,
    max_send,
    max_recv,
):
    slab = lax.axis_index("slab")
    sub = lax.axis_index("sub")
    around = (
        (1, 0),
        (-1, 0),
        (0, 1),
        (0, -1),
        (1, 1),
        (1, -1),
        (-1, 1),
        (-1, -1),
    )
    near = [((slab + u + NSLAB) % NSLAB, (sub + v + NSUB) % NSUB) for u, v in around]
    low, part = sub % HALF, sub // HALF
    line = [(slab, part * HALF + (low + d) % HALF) for d in LINE_STEPS]
    place = part * NSLAB + slab
    plane_peers = []
    for d in PLANE_STEPS:
        there = (place + d) % (NSLAB * 2)
        plane_peers.append((there % NSLAB, (there // NSLAB) * HALF + low))

    barrier = pltpu.get_barrier_semaphore()
    everyone = plane_peers + line + near
    for device in everyone:
        pl.semaphore_signal(barrier, inc=1, device_id=device, device_id_type=MESH)

    loads = [
        pltpu.make_async_copy(source, target, load_sem.at[k])
        for k, (source, target) in enumerate(
            ((off_in, off), (lab_in, lab), (par_in, par), (vel_in, vel), (anc_in, anc))
        )
    ]
    for copy in loads:
        copy.start()

    blank = jnp.zeros((PARTS, 8, 128), jnp.float32)

    def clear(q, carry):
        for e in range(4):
            box[e, q, :, 0:8, :] = blank
            box[e, q, :, 16:24, :] = blank
        labels[q, :, 0:8, :] = blank[:SLOTS]
        labels[q, :, 16:24, :] = blank[:SLOTS]
        return carry

    lax.fori_loop(0, 4, clear, 0)
    rows_out[...] = jnp.zeros(rows_out.shape, jnp.float32)

    loads[0].wait()
    loads[1].wait()
    for p in range(2):
        for j in range(SLOTS):
            label = lab[j, p]
            labels[p + 1, j, 8:16, :] = label.astype(jnp.float32)
            box[0, p + 1, j, 8:16, :] = off[0, j, p] + jnp.where(label < 0, away, 0.0)
            for c in (1, 2):
                box[0, p + 1, c * SLOTS + j, 8:16, :] = off[c, j, p]

    def pack(e, p):
        for side, row in ((0, 8), (1, 15)):
            for k in range(PARTS):
                rows_out[e, side, p, k : k + 1, :] = box[e, p + 1, k, row : row + 1, :]

    pack(0, 0)
    pack(0, 1)
    for side, row in ((0, 8), (1, 15)):
        for p in range(2):
            for j in range(SLOTS):
                rows_out[0, side, p, PARTS + j : PARTS + j + 1, :] = labels[
                    p + 1, j, row : row + 1, :
                ]

    loads[2].wait()

    def bonds(t, carry):
        p = t // 9
        g = t % 9
        for ez in range(3):
            for j in range(SLOTS):
                wanted = (g * 3 + ez) * SLOTS + j
                for i in range(SLOTS):
                    bond[p, g, ez, j, i] = jnp.where(par[0, i, p] == wanted, BOND, 0.0) + jnp.where(
                        par[1, i, p] == wanted, BOND, 0.0
                    )
        return carry

    lax.fori_loop(0, 18, bonds, 0)
    loads[3].wait()
    loads[4].wait()
    for p in range(2):
        for i in range(SLOTS):
            free[p, i] = jnp.where((lab[i, p] >= 0) & (anc[i, p] == 0), 1.0, 0.0)

    pl.semaphore_wait(barrier, len(everyone))

    def send(e, k, to, source, target):
        return pltpu.make_async_remote_copy(
            src_ref=source,
            dst_ref=target,
            send_sem=face_send.at[e, k],
            recv_sem=face_recv.at[e, k],
            device_id=near[around.index(to)],
            device_id_type=MESH,
        )

    def face(e, p):
        x = 2 * p - 1
        own, far = box.at[e, p + 1, :, 8:16, :], box.at[e, 3 - 3 * p, :, 8:16, :]
        return send(e, 5 * p, (x, 0), own, far)

    def edges(e, p):
        x, q = 2 * p - 1, 3 - 3 * p
        out = []
        for side, y in ((0, -1), (1, 1)):
            rows, here = rows_out.at[e, side, p], rows_in.at[e, 1 - side]
            out.append(send(e, 5 * p + 1 + side, (0, y), rows, here.at[p + 1]))
            out.append(send(e, 5 * p + 3 + side, (x, y), rows, here.at[q]))
        return out

    label_faces = [
        send(
            0,
            10 + p,
            (2 * p - 1, 0),
            labels.at[p + 1, :, 8:16, :],
            labels.at[3 - 3 * p, :, 8:16, :],
        )
        for p in range(2)
    ]
    face_copies = [[face(e, p) for p in range(2)] for e in range(4)]
    edge_copies = [[edges(e, p) for p in range(2)] for e in range(4)]

    def unpack(e, p):
        def one(t, carry):
            q = (1 + 2 * t) if p == 0 else (2 - 2 * t)
            for side, row in ((0, 7), (1, 16)):
                for k in range(PARTS):
                    box[e, q, k, row : row + 1, :] = rows_in[e, side, q, k : k + 1, :]
            return carry

        lax.fori_loop(0, 2, one, 0)

    def group(e, p, q, ey, fresh):
        ex = (q - p - 1).astype(jnp.float32) * cell_width
        g = 3 * (q - p) + (ey + 1)
        own = [
            [box[e, p + 1, c * SLOTS + i, 8:16, :] for i in range(SLOTS)] for c in range(3)
        ]
        total = [
            [
                jnp.zeros((8, 128), jnp.float32) if fresh else acc[p, c * SLOTS + i]
                for i in range(SLOTS)
            ]
            for c in range(3)
        ]
        own_x = [own[0][i] - ex for i in range(SLOTS)]
        own_y = [own[1][i] - ey * cell_width for i in range(SLOTS)]
        for ez in (-1, 0, 1):
            own_z = [own[2][i] - ez * cell_width for i in range(SLOTS)]
            for j in range(SLOTS):
                other = [box[e, q, c * SLOTS + j, 8 + ey : 16 + ey, :] for c in range(3)]
                if ez != 0:
                    other = [pltpu.roll(o, (-ez) % 128, 1) for o in other]
                for i in range(SLOTS):
                    sx = own_x[i] - other[0]
                    sy = own_y[i] - other[1]
                    sz = own_z[i] - other[2]
                    dist = sx * sx + sy * sy + sz * sz
                    least = soft_floor if e == 0 else floors[p, g, ez + 1, j, i]
                    q1 = pl.reciprocal(jnp.maximum(dist, least), approx=True)
                    q2 = q1 * q1
                    q3 = q2 * q1
                    q4 = q2 * q2
                    push = q4 * jnp.maximum(q3 - 0.5, 0.0)
                    pull = bond[p, g, ez + 1, j, i] * pl.reciprocal(
                        jnp.maximum(9.0 - dist, 1.8), approx=True
                    )
                    coef = push + pull
                    total[0][i] = total[0][i] + coef * sx
                    total[1][i] = total[1][i] + coef * sy
                    total[2][i] = total[2][i] + coef * sz
        for c in range(3):
            for i in range(SLOTS):
                acc[p, c * SLOTS + i] = total[c][i]

    def inner(e):
        def first(p, carry):
            group(e, p, p + 1, 0, True)
            return carry

        def second(p, carry):
            group(e, p, 2 - p, 0, False)
            return carry

        lax.fori_loop(0, 2, first, 0)
        lax.fori_loop(0, 2, second, 0)

    def sides(e, pairs):
        def one(t, carry):
            p, q = pairs(t)
            for ey in (-1, 1):
                group(e, p, q, ey, False)
            return carry

        return one

    def outer(e, p):
        for ey in (-1, 0, 1):
            group(e, p, 3 * p, ey, False)

    def limits():
        def one(t, carry):
            p = t // 3
            for ey in (-1, 0, 1):
                g = 3 * (t % 3) + (ey + 1)
                for ez in (-1, 0, 1):
                    for j in range(SLOTS):
                        other = labels[p + t % 3, j, 8 + ey : 16 + ey, :]
                        if ez != 0:
                            other = pltpu.roll(other, (-ez) % 128, 1)
                        for i in range(SLOTS):
                            floors[p, g, ez + 1, j, i] = jnp.where(
                                labels[p + 1, i, 8:16, :] == other, no_pair, soft_floor
                            )
            return carry

        lax.fori_loop(0, 6, one, 0)

    def global_max(r, value):
        row = jnp.max(value, axis=0, keepdims=True)
        base = 0
        for phase, peers in enumerate((line, plane_peers)):
            mine[r, phase] = row
            copies = [
                pltpu.make_async_remote_copy(
                    src_ref=mine.at[r, phase],
                    dst_ref=slots.at[r, base + k],
                    send_sem=max_send.at[r, base + k],
                    recv_sem=max_recv.at[r, base + k],
                    device_id=device,
                    device_id_type=MESH,
                )
                for k, device in enumerate(peers)
            ]
            for copy in copies:
                copy.start()
            yield copies
            for copy in copies:
                copy.wait_recv()
            row = jnp.maximum(row, jnp.max(slots[r, base : base + len(peers)], axis=0))
            base += len(peers)
        yield jnp.max(row, axis=1, keepdims=True)

    for copy in face_copies[0] + edge_copies[0][0] + edge_copies[0][1] + label_faces:
        copy.start()
    inner(0)
    for p in range(2):
        for copy in edge_copies[0][p]:
            copy.wait_recv()
        unpack(0, p)
    for p in range(2):
        lax.fori_loop(0, 2, sides(0, lambda t: (jnp.int32(p), 1 + t)), 0)
        face_copies[0][1 - p].wait_recv()
        outer(0, jnp.int32(p))
        for c in range(3):
            for i in range(SLOTS):
                k = c * SLOTS + i
                force = acc[p, k] * FORCE_UNIT * free[p, i]
                moving = free[p, i] * vel[c, i, p]
                half_out[c, i, p] = moving + half_step * force
                box[1, p + 1, k, 8:16, :] = box[0, p + 1, k, 8:16, :] + (
                    time_step * moving + half_step_sq * force
                )
        face_copies[1][p].start()
        pack(1, p)
        for copy in edge_copies[1][p]:
            copy.start()
    for copy in label_faces:
        copy.wait_recv()

    def label_rows(q, carry):
        for side, row in ((0, 7), (1, 16)):
            for j in range(SLOTS):
                labels[q, j, row : row + 1, :] = rows_in[
                    0, side, q, PARTS + j : PARTS + j + 1, :
                ]
        return carry

    lax.fori_loop(0, 4, label_rows, 0)
    limits()
    inner(1)
    for p in range(2):
        for copy in edge_copies[1][p]:
            copy.wait_recv()
        unpack(1, p)
        lax.fori_loop(0, 2, sides(1, lambda t: (t, jnp.int32(p + 1))), 0)
        face_copies[1][p].wait_recv()
        outer(1, jnp.int32(1 - p))

    started = face_copies[0] + label_faces
    for e in range(2):
        started += edge_copies[e][0] + edge_copies[e][1]
    for r in range(3):
        if r > 0:
            inner(1)
            lax.fori_loop(0, 4, sides(1, lambda t: (t // 2, 1 + t % 2)), 0)

            def far(p, carry):
                outer(1, p)
                return carry

            lax.fori_loop(0, 2, far, 0)
        final = r == 2
        peak = jnp.zeros((8, 128), jnp.float32)
        for p in range(2):
            for i in range(SLOTS):
                size = jnp.zeros((8, 128), jnp.float32)
                for c in range(3):
                    k = c * SLOTS + i
                    force = acc[p, k] * FORCE_UNIT * free[p, i]
                    size = size + force * force
                    if final:
                        unit_out[c, i, p] = force
                    else:
                        box[r + 2, p + 1, k, 8:16, :] = force
                peak = jnp.maximum(peak, size)
        steps = global_max(r, peak)
        started += next(steps)
        if not final:
            for p in range(2):
                face_copies[r + 2][p].start()
                pack(r + 2, p)
                for copy in edge_copies[r + 2][p]:
                    copy.start()
                started += [face_copies[r + 2][p]] + edge_copies[r + 2][p]
        started += next(steps)
        if not final:
            for p in range(2):
                for copy in edge_copies[r + 2][p]:
                    copy.wait_recv()
                unpack(r + 2, p)
                face_copies[r + 2][p].wait_recv()
        largest = next(steps)
        inverse = 1.0 / (jnp.sqrt(largest) + tiny_eps)
        scale = step_length * inverse
        if not final:
            if r == 0:
                for copy in face_copies[1]:
                    copy.wait_send()

            def move(q, carry):
                box[1, q] = box[1, q] + scale * box[r + 2, q]
                return carry

            lax.fori_loop(0, 4, move, 0)
        else:
            for p in range(2):
                for c in range(3):
                    for i in range(SLOTS):
                        force = unit_out[c, i, p]
                        place_now = box[1, p + 1, c * SLOTS + i, 8:16, :] + scale * force
                        if c == 0:
                            place_now = jnp.where(lab[i, p] < 0, off[c, i, p], place_now)
                        pos_out[c, i, p] = place_now
                        unit_out[c, i, p] = inverse * force
    for copy in started:
        copy.wait_send()


def store(pos, half, unit, pos_out, half_out, unit_out, sem):
    copies = [
        pltpu.make_async_copy(source, target, sem.at[k])
        for k, (source, target) in enumerate(
            ((pos, pos_out), (half, half_out), (unit, unit_out))
        )
    ]
    for copy in copies:
        copy.start()
    for copy in copies:
        copy.wait()


def shards(offsets, velocities, chain_label, partners, anchored):
    f32 = jnp.float32
    shape = offsets.shape
    parts = pl.pallas_call(
        kernel,
        out_shape=(pltpu.VMEM(shape, f32),) * 3,
        in_specs=[pl.BlockSpec(memory_space=pl.ANY)] * 5,
        out_specs=[pl.BlockSpec(memory_space=pltpu.VMEM)] * 3,
        scratch_shapes=[
            pltpu.VMEM(shape, f32),
            pltpu.VMEM(shape, f32),
            pltpu.VMEM(chain_label.shape, jnp.int32),
            pltpu.VMEM(partners.shape, jnp.int32),
            pltpu.VMEM(anchored.shape, jnp.int32),
            pltpu.VMEM((4, 4, PARTS, 24, 128), f32),
            pltpu.VMEM((4, SLOTS, 24, 128), f32),
            pltpu.VMEM((4, 2, 2, 16, 128), f32),
            pltpu.VMEM((4, 2, 4, 16, 128), f32),
            pltpu.VMEM((2, 9, 3, SLOTS, SLOTS, 8, 128), f32),
            pltpu.VMEM((2, 9, 3, SLOTS, SLOTS, 8, 128), f32),
            pltpu.VMEM((2, PARTS, 8, 128), f32),
            pltpu.VMEM((2, SLOTS, 8, 128), f32),
            pltpu.VMEM((3, 2, 1, 128), f32),
            pltpu.VMEM((3, N1 + N2, 1, 128), f32),
            pltpu.SemaphoreType.DMA((5,)),
            pltpu.SemaphoreType.DMA((4, 12)),
            pltpu.SemaphoreType.DMA((4, 12)),
            pltpu.SemaphoreType.DMA((3, N1 + N2)),
            pltpu.SemaphoreType.DMA((3, N1 + N2)),
        ],
        compiler_params=pltpu.CompilerParams(
            collective_id=0, has_side_effects=True, vmem_limit_bytes=60 * 1024 * 1024
        ),
    )(offsets, velocities, chain_label, partners, anchored)
    return tuple(
        pl.pallas_call(
            store,
            out_shape=(jax.ShapeDtypeStruct(shape, f32),) * 3,
            in_specs=[pl.BlockSpec(memory_space=pl.ANY)] * 3,
            out_specs=[pl.BlockSpec(memory_space=pl.ANY)] * 3,
            scratch_shapes=[pltpu.SemaphoreType.DMA((3,))],
            compiler_params=pltpu.CompilerParams(vmem_limit_bytes=1024 * 1024),
        )(*parts)
    )


def solution(mesh):
    whole = P(None, None, "slab", "sub", None)
    labels = P(None, "slab", "sub", None)
    return jax.shard_map(
        shards,
        mesh=mesh,
        in_specs=(whole, whole, labels, whole, labels),
        out_specs=(whole, whole, whole),
        check_vma=False,
    )
```
